32 devices in a mesh: pole: 4 (over y, core), row: 4 (over z), col: 2 (over x).
Axes of the slice: x: 2, y: 2, z: 4, core: 2. Of those that a mesh axis runs over, the one named last changes fastest.
Arguments:
- h_diag: float32 [8, 128, 128], P(('row', 'col'), None, 'pole'), as said below
- h_off: float32 [8, 128, 128], P(('row', 'col'), None, 'pole'), as said below
- s_diag: float32 [8, 128, 128], P(('row', 'col'), None, 'pole'), as said below
- snode_size: int32 [8], replicated, may hold values from 32 to 128, as said below
- col_order: int32 [128], replicated, may hold values from 0 to 127, as said below
- shifts: float32 [8], P('pole'), as said below
- weights: float32 [8], P('pole'), may hold values from -0.45 to 0.45, as said below
Outputs:
- density_diag: float32 [8, 128, 128], P(('row', 'col'), None, 'pole')
- density_off: float32 [8, 128, 128], P(('row', 'col'), None, 'pole')
The draws below stay inside these ranges and needn't reach their ends.
Inputs may be any that keep to these rules, and one draw needn't show every extreme that they name: `snode_size`: rows and columns of a supernode at or beyond its live size are padding. Both ends of the range occur in every draw. `col_order`: each of 0 to 127 appears once. `h_diag`: with columns restored every block is symmetric, and for every nonnegative shift the shifted matrix is symmetric positive definite. `h_off`: couplings of the same shifted matrix. `s_diag`: with columns restored every block is symmetric positive definite. `shifts`: Positive, between 1 / 64 and 150 / 64. `weights`: magnitudes at least 0.08.
All inputs are finite; a program needn't handle non-finite values.
Results may differ from the reference program's by a relative error of at most 0.0002.
Values sent between devices are 32-bit elements; how exact they have to be, the bound alone decides.
A program may use at most 64 MiB of HBM per device.

```python
import jax
import jax.numpy as jnp
from jax import lax

SUPERNODE_WIDTH = 128
SUPERNODE_COUNT = 8
POLES = 8


def column_order(key):
    return jax.random.permutation(jax.random.fold_in(key, 71), SUPERNODE_WIDTH).astype(jnp.int32)


def live_sizes(key):
    sizes = jax.random.randint(jax.random.fold_in(key, 11), (SUPERNODE_COUNT,), SUPERNODE_WIDTH // 4, SUPERNODE_WIDTH + 1).astype(jnp.int32)
    return sizes.at[0].set(SUPERNODE_WIDTH).at[SUPERNODE_COUNT - 1].set(SUPERNODE_WIDTH // 4)


def orbital_signs(key):
    flips = jax.random.bernoulli(jax.random.fold_in(key, 73), 0.5, (SUPERNODE_COUNT + 1, SUPERNODE_WIDTH))
    return jnp.where(flips, 1.0, -1.0).astype(jnp.float32)


def dense_links(key):
    return jax.random.uniform(jax.random.fold_in(key, 83), (SUPERNODE_COUNT, SUPERNODE_WIDTH, SUPERNODE_WIDTH), jnp.float32, 0.0, 0.6 / SUPERNODE_WIDTH)


def inside(offset):
    return (jnp.arange(SUPERNODE_WIDTH) < SUPERNODE_WIDTH - offset).astype(jnp.float32)[None, :]


def later(values, offset):
    return jnp.concatenate([jnp.zeros((values.shape[0], offset), jnp.float32), values[:, :SUPERNODE_WIDTH - offset]], axis=1)


def band(values, offset):
    rows = jnp.arange(SUPERNODE_WIDTH)[:, None]
    cols = jnp.arange(SUPERNODE_WIDTH)[None, :]
    return jnp.where((cols - rows == offset)[None], values[:, :, None], 0.0)


def mirrored(first, second):
    upper = band(first, 1) + band(second, 2)
    return upper + jnp.swapaxes(upper, 1, 2)


def symmetric_dense(key, lowest, highest):
    raw = jax.random.uniform(key, (SUPERNODE_COUNT, SUPERNODE_WIDTH, SUPERNODE_WIDTH), jnp.float32, lowest, highest)
    off_diagonal = 1.0 - jnp.eye(SUPERNODE_WIDTH, dtype=jnp.float32)
    return 0.5 * (raw + jnp.swapaxes(raw, 1, 2)) * off_diagonal[None]


def coupling_blocks(key):
    key_main, key_up, key_down = jax.random.split(jax.random.fold_in(key, 79), 3)
    main = 2.0 - 0.0002 * jax.random.uniform(key_main, (SUPERNODE_COUNT, SUPERNODE_WIDTH), jnp.float32)
    upper = 0.3 - 3e-05 * jax.random.uniform(key_up, (SUPERNODE_COUNT, SUPERNODE_WIDTH), jnp.float32)
    lower = 0.3 - 3e-05 * jax.random.uniform(key_down, (SUPERNODE_COUNT, SUPERNODE_WIDTH), jnp.float32)
    return band(main, 0) + band(upper, 1) + jnp.swapaxes(band(lower, 1), 1, 2) + dense_links(key)


def arrive(blocks, order):
    return blocks[:, :, order]


def spread_log(key, shape, lowest, highest):
    span = jnp.log(highest / lowest)
    return lowest * jnp.exp(span * jax.random.uniform(key, shape, jnp.float32))


def draw_h_diag(key, part):
    order = column_order(key)
    signs = orbital_signs(key)
    links = dense_links(key)
    key = jax.random.fold_in(key, 3)
    near_low, near_high = (0.3, 0.9)
    far_low, far_high = (0.1, 0.3)
    margin_low, margin_high = (0.2, 2.0)
    cluster_lower, cluster_upper = (6.0, 16.0)
    key_closeby, key_distant, key_border, key_location, key_cluster, key_dense = jax.random.split(key, 6)
    near = jax.random.uniform(key_closeby, (SUPERNODE_COUNT, SUPERNODE_WIDTH), jnp.float32, near_low, near_high) * inside(1)
    far = jax.random.uniform(key_distant, (SUPERNODE_COUNT, SUPERNODE_WIDTH), jnp.float32, far_low, far_high) * inside(2)
    border_gap = spread_log(key_border, (SUPERNODE_COUNT, SUPERNODE_WIDTH), margin_low, margin_high) / (SUPERNODE_COUNT * SUPERNODE_COUNT)
    location_list = jax.random.randint(key_location, (3,), 0, SUPERNODE_COUNT)
    cluster_list = jnp.zeros((SUPERNODE_COUNT,), jnp.float32).at[location_list].set(1.0)
    border_gap = border_gap + cluster_list[:, None] * jax.random.uniform(key_cluster, (SUPERNODE_COUNT, SUPERNODE_WIDTH), jnp.float32, cluster_lower, cluster_upper) / SUPERNODE_COUNT
    intra_dense = symmetric_dense(key_dense, 0.0, 0.6 / SUPERNODE_WIDTH)
    link_rows = jnp.sum(links, axis=2)
    link_cols = jnp.roll(jnp.sum(links, axis=1), 1, axis=0)
    positions = jnp.arange(SUPERNODE_WIDTH)
    link_bound = 2.0 + 0.3 * (positions < SUPERNODE_WIDTH - 1).astype(jnp.float32) + 0.3 * (positions >= 1).astype(jnp.float32)
    intra_sum = near + later(near, 1) + far + later(far, 2) + jnp.sum(intra_dense, axis=2)
    diagonal = intra_sum + 2.0 * link_bound[None, :] + link_rows + link_cols + border_gap
    eye_matrix = jnp.eye(SUPERNODE_WIDTH, dtype=jnp.float32)
    gauge = signs[:SUPERNODE_COUNT, :, None] * signs[:SUPERNODE_COUNT, None, :]
    blocks = -gauge * (mirrored(near, far) + intra_dense) + diagonal[:, :, None] * eye_matrix[None]
    return arrive(blocks, order)


def draw_h_off(key, part):
    order = column_order(key)
    signs = orbital_signs(key)
    magnitude = coupling_blocks(key)
    blocks = -signs[:SUPERNODE_COUNT, :, None] * signs[1:, None, :] * magnitude
    return arrive(blocks, order)


def draw_s_diag(key, part):
    order = column_order(key)
    key = jax.random.fold_in(key, 7)
    scale_low, scale_high = (0.5, 2.0)
    key_scale, key_entry, key_closeby, key_distant, key_dense = jax.random.split(key, 5)
    block_scale = spread_log(key_scale, (SUPERNODE_COUNT, 1), scale_low, scale_high)
    diagonal = block_scale * jax.random.uniform(key_entry, (SUPERNODE_COUNT, SUPERNODE_WIDTH), jnp.float32, 0.6, 1.4)
    near = jax.random.uniform(key_closeby, (SUPERNODE_COUNT, SUPERNODE_WIDTH), jnp.float32, -0.1, 0.1) * inside(1)
    far = jax.random.uniform(key_distant, (SUPERNODE_COUNT, SUPERNODE_WIDTH), jnp.float32, -0.1, 0.1) * inside(2)
    dense_part = symmetric_dense(key_dense, -0.45 / SUPERNODE_WIDTH, 0.45 / SUPERNODE_WIDTH)
    root = jnp.sqrt(diagonal)
    eye_matrix = jnp.eye(SUPERNODE_WIDTH, dtype=jnp.float32)
    blocks = (mirrored(near, far) + dense_part) * root[:, :, None] * root[:, None, :] + diagonal[:, :, None] * eye_matrix[None]
    return arrive(blocks, order)


def stratified_log(key, offsets, highest):
    strata = jnp.arange(POLES).astype(jnp.float32)
    fraction = (strata + offsets) / POLES
    values = jnp.exp(jnp.log(highest) * fraction)
    arrangement = jax.random.permutation(key, POLES)
    return values[arrangement]


def draw_shifts(key, part):
    key = jax.random.fold_in(key, 13)
    key_offset, key_arrange = jax.random.split(key, 2)
    offsets = jax.random.uniform(key_offset, (POLES,), jnp.float32, 0.2, 0.8)
    return stratified_log(key_arrange, offsets, 150.0) / (SUPERNODE_COUNT * SUPERNODE_COUNT)


def draw_weights(key, part):
    key = jax.random.fold_in(key, 17)
    key_sign, key_size = jax.random.split(key, 2)
    magnitude = jax.random.uniform(key_size, (POLES,), jnp.float32, 0.1, 0.4)
    flips = jax.random.bernoulli(key_sign, 0.5, (POLES,))
    return jnp.where(flips, magnitude, -magnitude).astype(jnp.float32)


def draw_snode_size(key, part):
    return live_sizes(key)


def draw_col_order(key, part):
    return column_order(key)


def setup_inputs(seed: int = 0) -> dict:
    streams_of = jax.random.split(jax.random.key(seed), 8)
    return {
        "h_diag": draw_h_diag(jax.random.fold_in(streams_of[7], 71), 0),
        "h_off": draw_h_off(jax.random.fold_in(streams_of[7], 71), 0),
        "s_diag": draw_s_diag(jax.random.fold_in(streams_of[7], 71), 0),
        "snode_size": draw_snode_size(jax.random.fold_in(streams_of[7], 71), 0),
        "col_order": draw_col_order(jax.random.fold_in(streams_of[7], 71), 0),
        "shifts": draw_shifts(jax.random.fold_in(streams_of[7], 71), 0),
        "weights": draw_weights(jax.random.fold_in(streams_of[7], 71), 0),
    }


def lower_solve(factor, rhs):
    return lax.linalg.triangular_solve(factor, rhs, left_side=True, lower=True)

def upper_solve(factor, rhs):
    return lax.linalg.triangular_solve(factor, rhs, left_side=True, lower=True, transpose_a=True)

def transposed_product(left, right):
    return jnp.einsum('...ji,...jk->...ik', left, right, precision=lax.Precision.HIGHEST)

def product(left, right):
    return jnp.einsum('...ij,...jk->...ik', left, right, precision=lax.Precision.HIGHEST)

def restore(arrived, col_order):
    return jnp.zeros_like(arrived).at[:, :, col_order].set(arrived)

def reference(h_diag, h_off, s_diag, snode_size, col_order, shifts, weights):
    hamilton = restore(h_diag, col_order)
    coupling_raw = restore(h_off, col_order)
    intersection = restore(s_diag, col_order)
    widths = jnp.concatenate([snode_size.astype(jnp.int32), jnp.zeros((1,), jnp.int32)])
    positions = jnp.arange(SUPERNODE_WIDTH, dtype=jnp.int32)
    live_mask = (positions[None, :] < widths[:, None]).astype(jnp.float32)
    diag_mask = live_mask[:-1, :, None] * live_mask[:-1, None, :]
    link_mask = live_mask[:-1, :, None] * live_mask[1:, None, :]
    coupling = coupling_raw * link_mask
    earlier_links = jnp.concatenate([jnp.zeros((1, SUPERNODE_WIDTH, SUPERNODE_WIDTH), jnp.float32), coupling[:-1]], axis=0)
    identity_matrix = jnp.eye(SUPERNODE_WIDTH, dtype=jnp.float32)
    padding = identity_matrix * (1.0 - live_mask[:-1])[:, None, :]
    zero_block = jnp.zeros((SUPERNODE_WIDTH, SUPERNODE_WIDTH), jnp.float32)

    def one_pole(pole_shift):
        shifted = (hamilton + pole_shift * intersection) * diag_mask + padding

        def forward(carried, inputs):
            matrix, link = inputs
            factor = jnp.linalg.cholesky(matrix - carried)
            spread = lower_solve(factor, link)
            return (transposed_product(spread, spread), (carried, factor, spread))
        _, (left_states, factors, spreads) = lax.scan(forward, zero_block, (shifted, coupling))

        def backward(carried, inputs):
            matrix, link = inputs
            factor = jnp.linalg.cholesky(matrix - carried)
            spread = lower_solve(factor, jnp.swapaxes(link, 0, 1))
            return (transposed_product(spread, spread), carried)
        _, right_states = lax.scan(backward, zero_block, (shifted, earlier_links), reverse=True)

        def invert(matrix):
            factor = jnp.linalg.cholesky(matrix)
            half_inverse = lower_solve(factor, identity_matrix)
            return transposed_product(half_inverse, half_inverse)
        greens = lax.map(invert, shifted - left_states - right_states)
        successors = jnp.concatenate([greens[1:], zero_block[None]], axis=0)
        off_blocks = -product(upper_solve(factors, spreads), successors)
        return (greens, off_blocks)

    def accumulate(running, inputs):
        pole_shift, weight = inputs
        greens, off_blocks = one_pole(pole_shift)
        return ((running[0] + weight * greens, running[1] + weight * off_blocks), None)
    zeros_all = jnp.zeros((SUPERNODE_COUNT, SUPERNODE_WIDTH, SUPERNODE_WIDTH), jnp.float32)
    (total_diag, total_off), _ = lax.scan(accumulate, (zeros_all, zeros_all), (shifts, weights))
    density_diag = (total_diag * diag_mask)[:, :, col_order]
    density_off = (total_off * link_mask)[:, :, col_order]
    return (density_diag, density_off)
```

```python
import functools

import jax
import jax.numpy as jnp
from jax import lax
from jax.experimental import pallas as pl
from jax.experimental.pallas import tpu as pltpu
from jax.sharding import PartitionSpec as P

MESH = pl.DeviceIdType.MESH
N = 128
PANEL = 8


def dot(a, b):
    return lax.dot_general(
        a, b, (((1,), (0,)), ((), ())), precision=lax.Precision.HIGHEST,
        preferred_element_type=jnp.float32,
    )


def dot_t(a, b):
    return lax.dot_general(
        a, b, (((1,), (1,)), ((), ())), precision=lax.Precision.HIGHEST,
        preferred_element_type=jnp.float32,
    )


def lane(x, index):
    return jnp.take_along_axis(x, jnp.full(x.shape, index, jnp.int32), axis=1)


def invert(work, members):
    sub = lax.broadcasted_iota(jnp.int32, (PANEL, N), 0)
    lanes = lax.broadcasted_iota(jnp.int32, (PANEL, N), 1)

    def step(k, _):
        base = pl.multiple_of(k * PANEL, PANEL)
        inside = (lanes >= base) & (lanes < base + PANEL)
        for m in members:
            rows = work[m, pl.ds(base, PANEL), :]
            cols = [lane(rows, base + j) for j in range(PANEL)]
            rows = jnp.where(inside, jnp.where(lanes - base == sub, 1.0, 0.0), rows)
            for j in range(PANEL):
                pivot = sub == j
                r = 1.0 / jnp.broadcast_to(cols[j][j : j + 1], (PANEL, N))
                f = cols[j]

                def swept(x):
                    top = jnp.broadcast_to(x[j : j + 1], (PANEL, N))
                    return jnp.where(pivot, 0.0, x) - jnp.where(pivot, -top, f * top) * r

                cols = cols[: j + 1] + [swept(c) for c in cols[j + 1 :]]
                rows = swept(rows)
            tops = [jnp.broadcast_to(rows[j : j + 1], (PANEL, N)) for j in range(PANEL)]
            for t in range(N // PANEL):
                x = work[m, t * PANEL : (t + 1) * PANEL, :]
                parts = [lane(x, base + j) * tops[j] for j in range(PANEL)]
                while len(parts) > 1:
                    parts = [a + b for a, b in zip(parts[::2], parts[1::2])]
                work[m, t * PANEL : (t + 1) * PANEL, :] = jnp.where(inside, 0.0, x) - parts[0]
            work[m, pl.ds(base, PANEL), :] = rows
        return 0

    lax.fori_loop(0, N // PANEL, step, 0)


def kernel(
    n_pole, n_col, places, poles, levels,
    h_ref, o_ref, s_ref, size_ref, order_ref, shift_ref, weight_ref,
    diag_ref, off_ref,
    mixed, gathered, coupling_t, link_t, a_all, work, f_all, ul,
    send_l, send_r, recv_l, recv_r, g_send, g_recv, z_send, z_recv,
    gs, gr, cs, cr, ls, lr, rs, rr, ns, nr, zs, zr,
):
    q = lax.axis_index("pole")
    place = lax.axis_index("row") * n_col + lax.axis_index("col")
    share = N // n_pole

    def at(target):
        return {"row": target // n_col, "col": lax.rem(target, n_col)}

    def mate(o):
        return {"pole": lax.rem(q + o, n_pole)}

    distances = [1 << l for l in range(levels)]
    barrier = pltpu.get_barrier_semaphore()
    for o in range(1, n_pole):
        pl.semaphore_signal(barrier, inc=1, device_id=mate(o), device_id_type=MESH)
    count = n_pole - 1
    for d in distances:
        has_right = place + d < places
        has_left = place >= d

        @pl.when(has_right)
        def _():
            pl.semaphore_signal(barrier, inc=1, device_id=at(place + d), device_id_type=MESH)

        @pl.when(has_left)
        def _():
            pl.semaphore_signal(barrier, inc=1, device_id=at(place - d), device_id_type=MESH)

        count = count + has_right.astype(jnp.int32) + has_left.astype(jnp.int32)

    mixed[...] = jnp.zeros_like(mixed)
    mixed[:, 0:share] = h_ref[0]
    mixed[:, share : 2 * share] = o_ref[0]
    mixed[:, 2 * share : 3 * share] = s_ref[0]
    turned = mixed[...].T
    mine = pl.ds(pl.multiple_of(q * share, share), share)
    for i in range(3):
        gathered[mine, i * N : (i + 1) * N] = turned[i * share : (i + 1) * share]
    pl.semaphore_wait(barrier, count)
    copies = []
    for o in range(1, n_pole):
        copy = pltpu.make_async_remote_copy(
            src_ref=gathered.at[mine], dst_ref=gathered.at[mine],
            send_sem=gs.at[o - 1], recv_sem=gr.at[o - 1],
            device_id=mate(o), device_id_type=MESH,
        )
        copy.start()
        copies.append(copy)

    iota0 = lax.broadcasted_iota(jnp.int32, (N, N), 0)
    iota1 = lax.broadcasted_iota(jnp.int32, (N, N), 1)
    one_hot = jnp.where(iota0 == order_ref[...], 1.0, 0.0)
    size = size_ref[place]
    after = size_ref[jnp.minimum(place + 1, places - 1)]
    after = jnp.where(place + 1 < places, after, 0)
    diag_mask = (iota0 < size) & (iota1 < size)
    link_mask_t = (iota0 < after) & (iota1 < size)
    padding = jnp.where((iota0 == iota1) & (iota1 >= size), 1.0, 0.0)

    for copy in copies:
        copy.wait()
    restored = dot(one_hot, gathered[...])
    coupling_t[...] = jnp.where(link_mask_t, restored[:, N : 2 * N], 0.0)

    has_right = place + 1 < places
    has_left = place >= 1
    to_right = pltpu.make_async_remote_copy(
        src_ref=coupling_t, dst_ref=link_t, send_sem=cs, recv_sem=cr,
        device_id=at(jnp.minimum(place + 1, places - 1)), device_id_type=MESH,
    )

    @pl.when(has_right)
    def _():
        to_right.start()

    for p in range(poles):
        a = restored[:, :N] + shift_ref[p] * restored[:, 2 * N :]
        a = jnp.where(diag_mask, a, 0.0) + padding
        a_all[p] = a
        work[p] = a
        f_all[p] = jnp.zeros((N, N), jnp.float32)

    for level, d in enumerate(distances):
        last = level == levels - 1
        half = N if last else 2 * N
        invert(work, range(poles))
        if level == 0:
            @pl.when(has_left)
            def _():
                to_right.wait_recv()

            @pl.when(jnp.logical_not(has_left))
            def _():
                link_t[...] = jnp.zeros_like(link_t)

            for p in range(poles):
                ul[p, :N] = coupling_t[...]
                ul[p, N:] = link_t[...].T
        has_right_d = place + d < places
        has_left_d = place >= d
        rights, lefts = [], []
        for p in range(poles):
            if level:
                ul[p, :N] = recv_r[level - 1, p, :N]
                ul[p, N:] = recv_l[level - 1, p, N:]
            both = ul[p]
            product = dot(both, work[p])
            full = dot_t(product, both)
            send_r[level, p] = full[:, :N]
            send_l[level, p] = full[:, N:]
            right = pltpu.make_async_remote_copy(
                src_ref=send_r.at[level, p, pl.ds(0, half)],
                dst_ref=recv_l.at[level, p, pl.ds(0, half)],
                send_sem=rs.at[level, p], recv_sem=rr.at[level, p],
                device_id=at(jnp.minimum(place + d, places - 1)), device_id_type=MESH,
            )
            low = 2 * N - half
            left = pltpu.make_async_remote_copy(
                src_ref=send_l.at[level, p, pl.ds(low, half)],
                dst_ref=recv_r.at[level, p, pl.ds(low, half)],
                send_sem=ls.at[level, p], recv_sem=lr.at[level, p],
                device_id=at(jnp.maximum(place - d, 0)), device_id_type=MESH,
            )
            rights.append(right)
            lefts.append(left)

            @pl.when(has_right_d)
            def _():
                right.start()

            @pl.when(has_left_d)
            def _():
                left.start()

        @pl.when(jnp.logical_not(has_left_d))
        def _():
            recv_l[level] = jnp.zeros(recv_l.shape[1:], jnp.float32)

        @pl.when(jnp.logical_not(has_right_d))
        def _():
            recv_r[level] = jnp.zeros(recv_r.shape[1:], jnp.float32)

        for p in range(poles):
            @pl.when(has_left_d)
            def _():
                rights[p].wait_recv()

            @pl.when(has_right_d)
            def _():
                lefts[p].wait_recv()

            @pl.when(has_right_d)
            def _():
                rights[p].wait_send()

            @pl.when(has_left_d)
            def _():
                lefts[p].wait_send()

        for p in range(poles):
            f_all[p] += recv_l[level, p, :N]
            e = jnp.zeros((N, N), jnp.float32)
            for earlier in range(level + 1):
                e += recv_r[earlier, p, N:]
            work[p] = a_all[p] - f_all[p] - e

    @pl.when(has_right)
    def _():
        to_right.wait_send()

    for p in range(poles):
        work[poles + p] = a_all[p] - f_all[p]
    invert(work, range(2 * poles))

    total = jnp.zeros((N, N), jnp.float32)
    for p in range(poles):
        scaled = weight_ref[p] * work[p]
        g_send[p] = scaled
        total += scaled
    to_left = pltpu.make_async_remote_copy(
        src_ref=g_send, dst_ref=g_recv, send_sem=ns, recv_sem=nr,
        device_id=at(jnp.maximum(place - 1, 0)), device_id_type=MESH,
    )

    @pl.when(has_left)
    def _():
        to_left.start()

    halves = [dot(coupling_t[...], work[poles + p]) for p in range(poles)]
    order = one_hot.T
    z_send[:, :N] = dot(order, jnp.where(diag_mask, total, 0.0))

    @pl.when(has_right)
    def _():
        to_left.wait_recv()

    @pl.when(jnp.logical_not(has_right))
    def _():
        g_recv[...] = jnp.zeros_like(g_recv)

    off_t = jnp.zeros((N, N), jnp.float32)
    for p in range(poles):
        off_t -= dot(g_recv[p], halves[p])
    z_send[:, N:] = dot(order, jnp.where(link_mask_t, off_t, 0.0))

    copies = []
    for o in range(1, n_pole):
        theirs = pl.ds(pl.multiple_of(lax.rem(q + o, n_pole) * share, share), share)
        copy = pltpu.make_async_remote_copy(
            src_ref=z_send.at[theirs], dst_ref=z_recv.at[o - 1],
            send_sem=zs.at[o - 1], recv_sem=zr.at[o - 1],
            device_id=mate(o), device_id_type=MESH,
        )
        copy.start()
        copies.append(copy)

    @pl.when(has_left)
    def _():
        to_left.wait_send()

    result = z_send[mine]
    for o in range(1, n_pole):
        copies[o - 1].wait()
        result += z_recv[o - 1]
    mixed[0:share] = result[:, :N]
    mixed[share : 2 * share] = result[:, N:]
    turned = mixed[...].T
    diag_ref[0] = turned[:, :share]
    off_ref[0] = turned[:, share : 2 * share]


def solution(mesh):
    n_pole, n_row, n_col = (mesh.shape[a] for a in ("pole", "row", "col"))
    places = n_row * n_col
    levels = (places - 1).bit_length()

    def per_device(h_diag, h_off, s_diag, snode_size, col_order, shifts, weights):
        poles = shifts.shape[0]
        share = h_diag.shape[2]
        vmem = pl.BlockSpec(memory_space=pltpu.VMEM)
        smem = pl.BlockSpec(memory_space=pltpu.SMEM)
        f32 = functools.partial(lambda *shape: pltpu.VMEM(shape, jnp.float32))
        dma = pltpu.SemaphoreType.DMA
        message = f32(levels, poles, 2 * N, N)
        return tuple(
            pl.pallas_call(
                functools.partial(kernel, n_pole, n_col, places, poles, levels),
                out_shape=[jax.ShapeDtypeStruct((1, N, share), jnp.float32)] * 2,
                in_specs=[vmem, vmem, vmem, smem, vmem, smem, smem],
                out_specs=[vmem, vmem],
                scratch_shapes=[
                    f32(N, N), f32(N, 3 * N), f32(N, N), f32(N, N), f32(poles, N, N),
                    f32(2 * poles, N, N), f32(poles, N, N), f32(poles, 2 * N, N),
                    message, message, message, message,
                    f32(poles, N, N), f32(poles, N, N), f32(N, 2 * N),
                    f32(n_pole - 1, share, 2 * N),
                    dma((n_pole - 1,)), dma((n_pole - 1,)), dma, dma,
                    dma((levels, poles)), dma((levels, poles)),
                    dma((levels, poles)), dma((levels, poles)),
                    dma, dma, dma((n_pole - 1,)), dma((n_pole - 1,)),
                ],
                compiler_params=pltpu.CompilerParams(
                    collective_id=0, has_side_effects=True,
                    vmem_limit_bytes=32 * 1024 * 1024,
                ),
            )(h_diag, h_off, s_diag, snode_size, col_order.reshape(1, N), shifts, weights)
        )

    spread = P(("row", "col"), None, "pole")
    return jax.shard_map(
        per_device,
        mesh=mesh,
        in_specs=(spread, spread, spread, P(), P(), P("pole"), P("pole")),
        out_specs=(spread, spread),
        check_vma=False,
    )
```

```python
import functools

import jax
import jax.numpy as jnp
from jax import lax
from jax.experimental import pallas as pl
from jax.experimental.pallas import tpu as pltpu
from jax.sharding import PartitionSpec as P

MESH = pl.DeviceIdType.MESH
N = 128
PANEL = 16


def dot(a, b):
    return lax.dot_general(
        a, b, (((1,), (0,)), ((), ())), precision=lax.Precision.HIGHEST,
        preferred_element_type=jnp.float32,
    )


def dot_t(a, b):
    return lax.dot_general(
        a, b, (((1,), (1,)), ((), ())), precision=lax.Precision.HIGHEST,
        preferred_element_type=jnp.float32,
    )


def lane(x, index):
    return jnp.take_along_axis(x, jnp.full(x.shape, index, jnp.int32), axis=1)


def reciprocal(x):
    r = pl.reciprocal(x, approx=True)
    r = r * (2.0 - x * r)
    return r * (2.0 - x * r)


def eliminate(rows, cols, sub):
    shape = (PANEL, N)
    members = range(len(rows))
    for j in range(PANEL):
        pivot = sub == j
        tops = [
            [jnp.broadcast_to(cols[m][i][j : j + 1], shape) for i in range(j, PANEL)]
            for m in members
        ]
        scale = [
            jnp.concatenate([reciprocal(tops[m][0][:8])] * (PANEL // 8), axis=0) for m in members
        ]
        ends = [jnp.broadcast_to(rows[m][j : j + 1], shape) for m in members]
        fs = [jnp.where(pivot, -1.0, cols[m][j]) for m in members]
        for i in range(j + 1, PANEL):
            for m in members:
                cols[m][i] = (
                    jnp.where(pivot, 0.0, cols[m][i]) - (fs[m] * tops[m][i - j]) * scale[m]
                )
        for m in members:
            rows[m] = jnp.where(pivot, 0.0, rows[m]) - (fs[m] * ends[m]) * scale[m]
    return rows


def invert(work, members):
    sub = lax.broadcasted_iota(jnp.int32, (PANEL, N), 0)
    lanes = lax.broadcasted_iota(jnp.int32, (PANEL, N), 1)
    all_subs = lax.broadcasted_iota(jnp.int32, (N, N), 0)
    all_lanes = lax.broadcasted_iota(jnp.int32, (N, N), 1)

    def step(k, _):
        base = pl.multiple_of(k * PANEL, PANEL)
        rows = [work[m, pl.ds(base, PANEL), :] for m in members]
        inside = (lanes >= base) & (lanes < base + PANEL)
        cols = [[lane(r, base + j) for j in range(PANEL)] for r in rows]
        unit = jnp.where(lanes - base == sub, 1.0, 0.0)
        done = eliminate([jnp.where(inside, unit, r) for r in rows], cols, sub)
        panel_lanes = (all_lanes >= base) & (all_lanes < base + PANEL)
        panel_subs = (all_subs >= base) & (all_subs < base + PANEL)
        outs = []
        for i, m in enumerate(members):
            x = work[m]
            tall = jnp.concatenate([done[i]] * (N // PANEL), axis=0)
            left = jnp.where(panel_lanes, x, 0.0)
            rest = x - left - dot(left, jnp.where(panel_subs, tall, 0.0))
            outs.append(jnp.where(panel_subs, tall, rest))
        for i, m in enumerate(members):
            work[m] = outs[i]
        return 0

    lax.fori_loop(0, N // PANEL, step, 0)


def kernel(
    n_pole, n_col, places, poles, levels,
    h_ref, o_ref, s_ref, size_ref, order_ref, shift_ref, weight_ref,
    diag_ref, off_ref,
    mixed, gathered, coupling_t, link_t, a_all, work, f_all, ul,
    send_l, send_r, recv_l, recv_r, g_send, g_recv, z_send, z_recv,
    gs, gr, cs, cr, ls, lr, rs, rr, ns, nr, zs, zr,
):
    q = lax.axis_index("pole")
    place = lax.axis_index("row") * n_col + lax.axis_index("col")
    share = N // n_pole

    def at(target):
        return {"row": target // n_col, "col": lax.rem(target, n_col)}

    def mate(o):
        return {"pole": lax.rem(q + o, n_pole)}

    distances = [1 << l for l in range(levels)]
    barrier = pltpu.get_barrier_semaphore()
    for o in range(1, n_pole):
        pl.semaphore_signal(barrier, inc=1, device_id=mate(o), device_id_type=MESH)
    count = n_pole - 1
    for d in distances:
        has_right = place + d < places
        has_left = place >= d

        @pl.when(has_right)
        def _():
            pl.semaphore_signal(barrier, inc=1, device_id=at(place + d), device_id_type=MESH)

        @pl.when(has_left)
        def _():
            pl.semaphore_signal(barrier, inc=1, device_id=at(place - d), device_id_type=MESH)

        count = count + has_right.astype(jnp.int32) + has_left.astype(jnp.int32)

    mixed[...] = jnp.zeros_like(mixed)
    mixed[:, 0:share] = h_ref[0]
    mixed[:, share : 2 * share] = o_ref[0]
    mixed[:, 2 * share : 3 * share] = s_ref[0]
    turned = mixed[...].T
    mine = pl.ds(pl.multiple_of(q * share, share), share)
    for i in range(3):
        gathered[mine, i * N : (i + 1) * N] = turned[i * share : (i + 1) * share]
    pl.semaphore_wait(barrier, count)
    copies = []
    for o in range(1, n_pole):
        copy = pltpu.make_async_remote_copy(
            src_ref=gathered.at[mine], dst_ref=gathered.at[mine],
            send_sem=gs.at[o - 1], recv_sem=gr.at[o - 1],
            device_id=mate(o), device_id_type=MESH,
        )
        copy.start()
        copies.append(copy)

    iota0 = lax.broadcasted_iota(jnp.int32, (N, N), 0)
    iota1 = lax.broadcasted_iota(jnp.int32, (N, N), 1)
    one_hot = jnp.where(iota0 == order_ref[...], 1.0, 0.0)
    size = size_ref[place]
    after = size_ref[jnp.minimum(place + 1, places - 1)]
    after = jnp.where(place + 1 < places, after, 0)
    diag_mask = (iota0 < size) & (iota1 < size)
    link_mask_t = (iota0 < after) & (iota1 < size)
    padding = jnp.where((iota0 == iota1) & (iota1 >= size), 1.0, 0.0)

    for copy in copies:
        copy.wait()
    restored = dot(one_hot, gathered[...])
    coupling_t[...] = jnp.where(link_mask_t, restored[:, N : 2 * N], 0.0)

    has_right = place + 1 < places
    has_left = place >= 1
    to_right = pltpu.make_async_remote_copy(
        src_ref=coupling_t, dst_ref=link_t, send_sem=cs, recv_sem=cr,
        device_id=at(jnp.minimum(place + 1, places - 1)), device_id_type=MESH,
    )

    @pl.when(has_right)
    def _():
        to_right.start()

    for p in range(poles):
        a = restored[:, :N] + shift_ref[p] * restored[:, 2 * N :]
        a = jnp.where(diag_mask, a, 0.0) + padding
        a_all[p] = a
        work[p] = a
        f_all[p] = jnp.zeros((N, N), jnp.float32)

    for level, d in enumerate(distances):
        last = level == levels - 1
        half = N if last else 2 * N
        invert(work, range(poles))
        if level == 0:
            @pl.when(has_left)
            def _():
                to_right.wait_recv()

            @pl.when(jnp.logical_not(has_left))
            def _():
                link_t[...] = jnp.zeros_like(link_t)

            for p in range(poles):
                ul[p, :N] = coupling_t[...]
                ul[p, N:] = link_t[...].T
        has_right_d = place + d < places
        has_left_d = place >= d
        rights, lefts = [], []
        for p in range(poles):
            if level:
                ul[p, :N] = recv_r[level - 1, p, :N]
                ul[p, N:] = recv_l[level - 1, p, N:]
            both = ul[p]
            product = dot(both, work[p])
            full = dot_t(product, both)
            send_r[level, p] = full[:, :N]
            send_l[level, p] = full[:, N:]
            right = pltpu.make_async_remote_copy(
                src_ref=send_r.at[level, p, pl.ds(0, half)],
                dst_ref=recv_l.at[level, p, pl.ds(0, half)],
                send_sem=rs.at[level, p], recv_sem=rr.at[level, p],
                device_id=at(jnp.minimum(place + d, places - 1)), device_id_type=MESH,
            )
            low = 2 * N - half
            left = pltpu.make_async_remote_copy(
                src_ref=send_l.at[level, p, pl.ds(low, half)],
                dst_ref=recv_r.at[level, p, pl.ds(low, half)],
                send_sem=ls.at[level, p], recv_sem=lr.at[level, p],
                device_id=at(jnp.maximum(place - d, 0)), device_id_type=MESH,
            )
            rights.append(right)
            lefts.append(left)

            @pl.when(has_right_d)
            def _():
                right.start()

            @pl.when(has_left_d)
            def _():
                left.start()

        @pl.when(jnp.logical_not(has_left_d))
        def _():
            recv_l[level] = jnp.zeros(recv_l.shape[1:], jnp.float32)

        @pl.when(jnp.logical_not(has_right_d))
        def _():
            recv_r[level] = jnp.zeros(recv_r.shape[1:], jnp.float32)

        for p in range(poles):
            @pl.when(has_left_d)
            def _():
                rights[p].wait_recv()

            @pl.when(has_right_d)
            def _():
                lefts[p].wait_recv()

            @pl.when(has_right_d)
            def _():
                rights[p].wait_send()

            @pl.when(has_left_d)
            def _():
                lefts[p].wait_send()

        for p in range(poles):
            f_all[p] += recv_l[level, p, :N]
            e = jnp.zeros((N, N), jnp.float32)
            for earlier in range(level + 1):
                e += recv_r[earlier, p, N:]
            work[p] = a_all[p] - f_all[p] - e

    @pl.when(has_right)
    def _():
        to_right.wait_send()

    for p in range(poles):
        work[poles + p] = a_all[p] - f_all[p]
    invert(work, range(2 * poles))

    total = jnp.zeros((N, N), jnp.float32)
    for p in range(poles):
        scaled = weight_ref[p] * work[p]
        g_send[p] = scaled
        total += scaled
    to_left = pltpu.make_async_remote_copy(
        src_ref=g_send, dst_ref=g_recv, send_sem=ns, recv_sem=nr,
        device_id=at(jnp.maximum(place - 1, 0)), device_id_type=MESH,
    )

    @pl.when(has_left)
    def _():
        to_left.start()

    halves = [dot(coupling_t[...], work[poles + p]) for p in range(poles)]
    order = one_hot.T
    z_send[:, :N] = dot(order, jnp.where(diag_mask, total, 0.0))

    @pl.when(has_right)
    def _():
        to_left.wait_recv()

    @pl.when(jnp.logical_not(has_right))
    def _():
        g_recv[...] = jnp.zeros_like(g_recv)

    off_t = jnp.zeros((N, N), jnp.float32)
    for p in range(poles):
        off_t -= dot(g_recv[p], halves[p])
    z_send[:, N:] = dot(order, jnp.where(link_mask_t, off_t, 0.0))

    copies = []
    for o in range(1, n_pole):
        theirs = pl.ds(pl.multiple_of(lax.rem(q + o, n_pole) * share, share), share)
        copy = pltpu.make_async_remote_copy(
            src_ref=z_send.at[theirs], dst_ref=z_recv.at[o - 1],
            send_sem=zs.at[o - 1], recv_sem=zr.at[o - 1],
            device_id=mate(o), device_id_type=MESH,
        )
        copy.start()
        copies.append(copy)

    @pl.when(has_left)
    def _():
        to_left.wait_send()

    result = z_send[mine]
    for o in range(1, n_pole):
        copies[o - 1].wait()
        result += z_recv[o - 1]
    mixed[0:share] = result[:, :N]
    mixed[share : 2 * share] = result[:, N:]
    turned = mixed[...].T
    diag_ref[0] = turned[:, :share]
    off_ref[0] = turned[:, share : 2 * share]


def solution(mesh):
    n_pole, n_row, n_col = (mesh.shape[a] for a in ("pole", "row", "col"))
    places = n_row * n_col
    levels = (places - 1).bit_length()

    def per_device(h_diag, h_off, s_diag, snode_size, col_order, shifts, weights):
        poles = shifts.shape[0]
        share = h_diag.shape[2]
        vmem = pl.BlockSpec(memory_space=pltpu.VMEM)
        smem = pl.BlockSpec(memory_space=pltpu.SMEM)
        f32 = functools.partial(lambda *shape: pltpu.VMEM(shape, jnp.float32))
        dma = pltpu.SemaphoreType.DMA
        message = f32(levels, poles, 2 * N, N)
        return tuple(
            pl.pallas_call(
                functools.partial(kernel, n_pole, n_col, places, poles, levels),
                out_shape=[jax.ShapeDtypeStruct((1, N, share), jnp.float32)] * 2,
                in_specs=[vmem, vmem, vmem, smem, vmem, smem, smem],
                out_specs=[vmem, vmem],
                scratch_shapes=[
                    f32(N, N), f32(N, 3 * N), f32(N, N), f32(N, N), f32(poles, N, N),
                    f32(2 * poles, N, N), f32(poles, N, N), f32(poles, 2 * N, N),
                    message, message, message, message,
                    f32(poles, N, N), f32(poles, N, N), f32(N, 2 * N),
                    f32(n_pole - 1, share, 2 * N),
                    dma((n_pole - 1,)), dma((n_pole - 1,)), dma, dma,
                    dma((levels, poles)), dma((levels, poles)),
                    dma((levels, poles)), dma((levels, poles)),
                    dma, dma, dma((n_pole - 1,)), dma((n_pole - 1,)),
                ],
                compiler_params=pltpu.CompilerParams(
                    collective_id=0, has_side_effects=True,
                    vmem_limit_bytes=32 * 1024 * 1024,
                ),
            )(h_diag, h_off, s_diag, snode_size, col_order.reshape(1, N), shifts, weights)
        )

    spread = P(("row", "col"), None, "pole")
    return jax.shard_map(
        per_device,
        mesh=mesh,
        in_specs=(spread, spread, spread, P(), P(), P("pole"), P("pole")),
        out_specs=(spread, spread),
        check_vma=False,
    )
```

```python
import functools

import jax
import jax.numpy as jnp
from jax import lax
from jax.experimental import pallas as pl
from jax.experimental.pallas import tpu as pltpu
from jax.sharding import PartitionSpec as P

MESH = pl.DeviceIdType.MESH
N = 128
PANEL = 16


def dot(a, b):
    return lax.dot_general(
        a, b, (((1,), (0,)), ((), ())), precision=lax.Precision.HIGHEST,
        preferred_element_type=jnp.float32,
    )


def dot_t(a, b):
    return lax.dot_general(
        a, b, (((1,), (1,)), ((), ())), precision=lax.Precision.HIGHEST,
        preferred_element_type=jnp.float32,
    )


def lane(x, index):
    return jnp.take_along_axis(x, jnp.full(x.shape, index, jnp.int32), axis=1)


def reciprocal(x):
    r = pl.reciprocal(x, approx=True)
    return r * (2.0 - x * r)


def eliminate(rows, cols, sub):
    shape = (PANEL, N)
    members = range(len(rows))
    for j in range(PANEL):
        pivot = sub == j
        tops = [
            [jnp.broadcast_to(cols[m][i][j : j + 1], shape) for i in range(j, PANEL)]
            for m in members
        ]
        scale = [
            jnp.concatenate([reciprocal(tops[m][0][:8])] * (PANEL // 8), axis=0) for m in members
        ]
        ends = [jnp.broadcast_to(rows[m][j : j + 1], shape) for m in members]
        fs = [jnp.where(pivot, -1.0, cols[m][j]) for m in members]
        for i in range(j + 1, PANEL):
            for m in members:
                cols[m][i] = (
                    jnp.where(pivot, 0.0, cols[m][i]) - (fs[m] * tops[m][i - j]) * scale[m]
                )
        for m in members:
            rows[m] = jnp.where(pivot, 0.0, rows[m]) - (fs[m] * ends[m]) * scale[m]
    return rows


def invert(work, members):
    sub = lax.broadcasted_iota(jnp.int32, (PANEL, N), 0)
    lanes = lax.broadcasted_iota(jnp.int32, (PANEL, N), 1)
    all_subs = lax.broadcasted_iota(jnp.int32, (N, N), 0)
    all_lanes = lax.broadcasted_iota(jnp.int32, (N, N), 1)

    def step(k, _):
        base = pl.multiple_of(k * PANEL, PANEL)
        rows = [work[m, pl.ds(base, PANEL), :] for m in members]
        inside = (lanes >= base) & (lanes < base + PANEL)
        cols = [[lane(r, base + j) for j in range(PANEL)] for r in rows]
        unit = jnp.where(lanes - base == sub, 1.0, 0.0)
        done = eliminate([jnp.where(inside, unit, r) for r in rows], cols, sub)
        panel_lanes = (all_lanes >= base) & (all_lanes < base + PANEL)
        panel_subs = (all_subs >= base) & (all_subs < base + PANEL)
        outs = []
        for i, m in enumerate(members):
            x = work[m]
            tall = jnp.concatenate([done[i]] * (N // PANEL), axis=0)
            left = jnp.where(panel_lanes, x, 0.0)
            rest = x - left - dot(left, jnp.where(panel_subs, tall, 0.0))
            outs.append(jnp.where(panel_subs, tall, rest))
        for i, m in enumerate(members):
            work[m] = outs[i]
        return 0

    lax.fori_loop(0, N // PANEL, step, 0)


def kernel(
    n_pole, n_col, places, poles, levels,
    h_ref, o_ref, s_ref, size_ref, order_ref, shift_ref, weight_ref,
    diag_ref, off_ref,
    gathered, coupling_t, link_t, a_all, work, f_all, d_all, ul,
    t_send, t_recv, n_send, n_recv, g_send, g_recv, z_send, z_recv,
    gs, gr, cs, cr, ts, tr, xs, xr, ns, nr, zs, zr,
):
    q = lax.axis_index("pole")
    place = lax.axis_index("row") * n_col + lax.axis_index("col")
    share = N // n_pole

    def at(target):
        return {"row": target // n_col, "col": lax.rem(target, n_col)}

    def mate(o):
        return {"pole": lax.rem(q + o, n_pole)}

    distances = [1 << l for l in range(levels)]
    barrier = pltpu.get_barrier_semaphore()
    for o in range(1, n_pole):
        pl.semaphore_signal(barrier, inc=1, device_id=mate(o), device_id_type=MESH)
    count = n_pole - 1
    for d in distances:
        has_right = place + d < places
        has_left = place >= d

        @pl.when(has_right)
        def _():
            pl.semaphore_signal(barrier, inc=1, device_id=at(place + d), device_id_type=MESH)

        @pl.when(has_left)
        def _():
            pl.semaphore_signal(barrier, inc=1, device_id=at(place - d), device_id_type=MESH)

        count = count + has_right.astype(jnp.int32) + has_left.astype(jnp.int32)

    mine = pl.ds(pl.multiple_of(q * share, share), share)
    for i, block in enumerate((h_ref, o_ref, s_ref)):
        gathered[mine, i * N : (i + 1) * N] = block[0]
    pl.semaphore_wait(barrier, count)
    copies = []
    for o in range(1, n_pole):
        copy = pltpu.make_async_remote_copy(
            src_ref=gathered.at[mine], dst_ref=gathered.at[mine],
            send_sem=gs.at[o - 1], recv_sem=gr.at[o - 1],
            device_id=mate(o), device_id_type=MESH,
        )
        copy.start()
        copies.append(copy)

    iota0 = lax.broadcasted_iota(jnp.int32, (N, N), 0)
    iota1 = lax.broadcasted_iota(jnp.int32, (N, N), 1)
    one_hot = jnp.where(iota0 == order_ref[...], 1.0, 0.0)
    size = size_ref[place]
    after = size_ref[jnp.minimum(place + 1, places - 1)]
    after = jnp.where(place + 1 < places, after, 0)
    diag_mask = (iota0 < size) & (iota1 < size)
    link_mask_t = (iota0 < after) & (iota1 < size)
    padding = jnp.where((iota0 == iota1) & (iota1 >= size), 1.0, 0.0)

    for copy in copies:
        copy.wait()
    restored = dot(one_hot, gathered[...])
    coupling_t[...] = jnp.where(link_mask_t, restored[:, N : 2 * N], 0.0)

    has_right = place + 1 < places
    has_left = place >= 1
    to_right = pltpu.make_async_remote_copy(
        src_ref=coupling_t, dst_ref=link_t, send_sem=cs, recv_sem=cr,
        device_id=at(jnp.minimum(place + 1, places - 1)), device_id_type=MESH,
    )

    @pl.when(has_right)
    def _():
        to_right.start()

    for p in range(poles):
        a = restored[:, :N] + shift_ref[p] * restored[:, 2 * N :]
        a = jnp.where(diag_mask, a, 0.0) + padding
        a_all[p] = a
        work[p] = a
        d_all[p] = a
        f_all[p] = jnp.zeros((N, N), jnp.float32)

    def exists(d):
        return place + d < places, place >= d

    def neighbour(d):
        return at(jnp.minimum(place + d, places - 1)), at(jnp.maximum(place - d, 0))

    def transfer(source, target, send, recv, d, side, slot):
        return pltpu.make_async_remote_copy(
            src_ref=source.at[(side, *slot)], dst_ref=target.at[(1 - side, *slot)],
            send_sem=send.at[(side, *slot)], recv_sem=recv.at[(1 - side, *slot)],
            device_id=neighbour(d)[side], device_id_type=MESH,
        )

    def start(copies, d):
        for side, copy in copies:
            pl.when(exists(d)[side])(copy.start)

    def finish(copies, d, target, level):
        for side in (0, 1):
            @pl.when(jnp.logical_not(exists(d)[side]))
            def _():
                target[side, level] = jnp.zeros(target.shape[2:], jnp.float32)

        for side, copy in copies:
            pl.when(exists(d)[1 - side])(copy.wait_recv)
            pl.when(exists(d)[side])(copy.wait_send)

    crossing = None
    for level, d in enumerate(distances):
        invert(work, range(poles))
        if level == 0:
            @pl.when(has_left)
            def _():
                to_right.wait_recv()

            @pl.when(jnp.logical_not(has_left))
            def _():
                link_t[...] = jnp.zeros_like(link_t)

            link = link_t[...].T
            for p in range(poles):
                ul[p, :N] = coupling_t[...]
                ul[p, N:] = link
        else:
            finish(crossing, distances[level - 1], n_recv, level - 1)
            for p in range(poles):
                ul[p, :N] = n_recv[0, level - 1, p]
                ul[p, N:] = n_recv[1, level - 1, p]
        products, terms = [], []
        for p in range(poles):
            both = ul[p]
            product = dot(both, work[p])
            products.append(product)
            for side in (0, 1):
                half = slice(side * N, (side + 1) * N)
                t_send[side, level, p] = dot_t(product[half], both[half])
                copy = transfer(t_send, t_recv, ts, tr, d, side, (level, p))
                terms.append((side, copy))
                start([(side, copy)], d)
        crossing = []
        if level < levels - 1:
            for p in range(poles):
                both = ul[p]
                n_send[0, level, p] = dot_t(products[p][N:], both[:N])
                n_send[1, level, p] = dot_t(products[p][:N], both[N:])
                for side in (0, 1):
                    copy = transfer(n_send, n_recv, xs, xr, d, side, (level, p))
                    crossing.append((side, copy))
                    start([(side, copy)], d)
        finish(terms, d, t_recv, level)
        for p in range(poles):
            f_all[p] += t_recv[1, level, p]
            left = d_all[p] - (t_recv[0, level, p] + t_recv[1, level, p])
            d_all[p] = left
            work[p] = left

    @pl.when(has_right)
    def _():
        to_right.wait_send()

    for p in range(poles):
        work[poles + p] = a_all[p] - f_all[p]
    invert(work, range(2 * poles))

    total = jnp.zeros((N, N), jnp.float32)
    for p in range(poles):
        scaled = weight_ref[p] * work[p]
        g_send[p] = scaled
        total += scaled
    to_left = pltpu.make_async_remote_copy(
        src_ref=g_send, dst_ref=g_recv, send_sem=ns, recv_sem=nr,
        device_id=at(jnp.maximum(place - 1, 0)), device_id_type=MESH,
    )

    @pl.when(has_left)
    def _():
        to_left.start()

    halves = [dot(coupling_t[...], work[poles + p]) for p in range(poles)]
    order = one_hot.T
    z_send[:, :N] = dot(order, jnp.where(diag_mask, total, 0.0))

    @pl.when(has_right)
    def _():
        to_left.wait_recv()

    @pl.when(jnp.logical_not(has_right))
    def _():
        g_recv[...] = jnp.zeros_like(g_recv)

    off_t = jnp.zeros((N, N), jnp.float32)
    for p in range(poles):
        off_t -= dot(g_recv[p], halves[p])
    z_send[:, N:] = dot(order, jnp.where(link_mask_t, off_t, 0.0))

    copies = []
    for o in range(1, n_pole):
        theirs = pl.ds(pl.multiple_of(lax.rem(q + o, n_pole) * share, share), share)
        copy = pltpu.make_async_remote_copy(
            src_ref=z_send.at[theirs], dst_ref=z_recv.at[o - 1],
            send_sem=zs.at[o - 1], recv_sem=zr.at[o - 1],
            device_id=mate(o), device_id_type=MESH,
        )
        copy.start()
        copies.append(copy)

    @pl.when(has_left)
    def _():
        to_left.wait_send()

    result = z_send[mine]
    for o in range(1, n_pole):
        copies[o - 1].wait()
        result += z_recv[o - 1]
    diag_ref[0] = result[:, :N]
    off_ref[0] = result[:, N:]


def solution(mesh):
    n_pole, n_row, n_col = (mesh.shape[a] for a in ("pole", "row", "col"))
    places = n_row * n_col
    levels = (places - 1).bit_length()

    def per_device(h_diag, h_off, s_diag, snode_size, col_order, shifts, weights):
        poles = shifts.shape[0]
        share = h_diag.shape[2]
        h_diag, h_off, s_diag = (jnp.swapaxes(x, 1, 2) for x in (h_diag, h_off, s_diag))
        vmem = pl.BlockSpec(memory_space=pltpu.VMEM)
        smem = pl.BlockSpec(memory_space=pltpu.SMEM)
        f32 = functools.partial(lambda *shape: pltpu.VMEM(shape, jnp.float32))
        dma = pltpu.SemaphoreType.DMA
        crossings = max(levels - 1, 1)
        results = pl.pallas_call(
            functools.partial(kernel, n_pole, n_col, places, poles, levels),
            out_shape=[jax.ShapeDtypeStruct((1, share, N), jnp.float32)] * 2,
            in_specs=[vmem, vmem, vmem, smem, vmem, smem, smem],
            out_specs=[vmem, vmem],
            scratch_shapes=[
                f32(N, 3 * N), f32(N, N), f32(N, N), f32(poles, N, N),
                f32(2 * poles, N, N), f32(poles, N, N), f32(poles, N, N),
                f32(poles, 2 * N, N),
                f32(2, levels, poles, N, N), f32(2, levels, poles, N, N),
                f32(2, crossings, poles, N, N), f32(2, crossings, poles, N, N),
                f32(poles, N, N), f32(poles, N, N), f32(N, 2 * N),
                f32(n_pole - 1, share, 2 * N),
                dma((n_pole - 1,)), dma((n_pole - 1,)), dma, dma,
                dma((2, levels, poles)), dma((2, levels, poles)),
                dma((2, crossings, poles)), dma((2, crossings, poles)),
                dma, dma, dma((n_pole - 1,)), dma((n_pole - 1,)),
            ],
            compiler_params=pltpu.CompilerParams(
                collective_id=0, has_side_effects=True,
                vmem_limit_bytes=32 * 1024 * 1024,
            ),
        )(h_diag, h_off, s_diag, snode_size, col_order.reshape(1, N), shifts, weights)
        return tuple(jnp.swapaxes(x, 1, 2) for x in results)

    spread = P(("row", "col"), None, "pole")
    return jax.shard_map(
        per_device,
        mesh=mesh,
        in_specs=(spread, spread, spread, P(), P(), P("pole"), P("pole")),
        out_specs=(spread, spread),
        check_vma=False,
    )
```

```python
import functools

import jax
import jax.numpy as jnp
from jax import lax
from jax.experimental import pallas as pl
from jax.experimental.pallas import tpu as pltpu
from jax.sharding import PartitionSpec as P

MESH = pl.DeviceIdType.MESH
N = 128
PANEL = 16


def dot(a, b):
    return lax.dot_general(
        a, b, (((1,), (0,)), ((), ())), precision=lax.Precision.HIGHEST,
        preferred_element_type=jnp.float32,
    )


def dot_t(a, b):
    return lax.dot_general(
        a, b, (((1,), (1,)), ((), ())), precision=lax.Precision.HIGHEST,
        preferred_element_type=jnp.float32,
    )


def lane(x, index):
    return jnp.take_along_axis(x, jnp.full(x.shape, index, jnp.int32), axis=1)


def reciprocal(x):
    r = pl.reciprocal(x, approx=True)
    return r * (2.0 - x * r)


def eliminate(rows, cols, sub):
    shape = (PANEL, N)
    members = range(len(rows))
    for j in range(PANEL):
        pivot = sub == j
        tops = [
            [jnp.broadcast_to(cols[m][i][j : j + 1], shape) for i in range(j, PANEL)]
            for m in members
        ]
        scale = [
            jnp.concatenate([reciprocal(tops[m][0][:8])] * (PANEL // 8), axis=0) for m in members
        ]
        ends = [jnp.broadcast_to(rows[m][j : j + 1], shape) for m in members]
        fs = [jnp.where(pivot, -1.0, cols[m][j]) for m in members]
        for i in range(j + 1, PANEL):
            for m in members:
                cols[m][i] = (
                    jnp.where(pivot, 0.0, cols[m][i]) - (fs[m] * tops[m][i - j]) * scale[m]
                )
        for m in members:
            rows[m] = jnp.where(pivot, 0.0, rows[m]) - (fs[m] * ends[m]) * scale[m]
    return rows


def invert(work, members):
    sub = lax.broadcasted_iota(jnp.int32, (PANEL, N), 0)
    lanes = lax.broadcasted_iota(jnp.int32, (PANEL, N), 1)
    all_subs = lax.broadcasted_iota(jnp.int32, (N, N), 0)
    all_lanes = lax.broadcasted_iota(jnp.int32, (N, N), 1)

    def step(k, _):
        base = pl.multiple_of(k * PANEL, PANEL)
        rows = [work[m, pl.ds(base, PANEL), :] for m in members]
        inside = (lanes >= base) & (lanes < base + PANEL)
        cols = [[lane(r, base + j) for j in range(PANEL)] for r in rows]
        unit = jnp.where(lanes - base == sub, 1.0, 0.0)
        done = eliminate([jnp.where(inside, unit, r) for r in rows], cols, sub)
        panel_lanes = (all_lanes >= base) & (all_lanes < base + PANEL)
        panel_subs = (all_subs >= base) & (all_subs < base + PANEL)
        outs = []
        for i, m in enumerate(members):
            x = work[m]
            tall = jnp.concatenate([done[i]] * (N // PANEL), axis=0)
            left = jnp.where(panel_lanes, x, 0.0)
            rest = x - left - dot(left, jnp.where(panel_subs, tall, 0.0))
            outs.append(jnp.where(panel_subs, tall, rest))
        for i, m in enumerate(members):
            work[m] = outs[i]
        return 0

    lax.fori_loop(0, N // PANEL, step, 0)


def pack(full):
    row = lax.broadcasted_iota(jnp.int32, (N // 2, N), 0)
    col = lax.broadcasted_iota(jnp.int32, (N // 2, N), 1)
    top, bottom = full[: N // 2], full[N // 2 :]
    body = jnp.where(row <= col, top, pltpu.roll(bottom, N // 2, 1))
    diagonal = jnp.sum(jnp.where(col == row + N // 2, bottom, 0.0), axis=0, keepdims=True)
    return body, jnp.broadcast_to(diagonal, (8, N))


def unpack(packed):
    row = lax.broadcasted_iota(jnp.int32, (N // 2, N), 0)
    col = lax.broadcasted_iota(jnp.int32, (N // 2, N), 1)
    body = packed[: N // 2]
    diagonal = jnp.broadcast_to(packed[N // 2 : N // 2 + 1], (N // 2, N))
    turned = jnp.concatenate([body, body], axis=0).T
    high, low = turned[: N // 2], turned[N // 2 :]
    top = jnp.where(row <= col, body, high)
    corner = jnp.where(
        col - N // 2 < row, pltpu.roll(body, N // 2, 1), pltpu.roll(high, N // 2, 1)
    )
    corner = jnp.where(col - N // 2 == row, diagonal, corner)
    return jnp.concatenate([top, jnp.where(col < N // 2, low, corner)], axis=0)


def kernel(
    n_pole, n_col, places, poles, levels,
    h_ref, o_ref, s_ref, size_ref, order_ref, shift_ref, weight_ref,
    diag_ref, off_ref,
    gathered, coupling_t, link_t, a_all, work, f_all, d_all, ul,
    t_send, t_recv, n_send, n_recv, g_send, g_recv, z_send, z_recv,
    gs, gr, cs, cr, ts, tr, xs, xr, ns, nr, zs, zr,
):
    q = lax.axis_index("pole")
    place = lax.axis_index("row") * n_col + lax.axis_index("col")
    share = N // n_pole

    def at(target):
        return {"row": target // n_col, "col": lax.rem(target, n_col)}

    def mate(o):
        return {"pole": lax.rem(q + o, n_pole)}

    distances = [1 << l for l in range(levels)]
    barrier = pltpu.get_barrier_semaphore()
    for o in range(1, n_pole):
        pl.semaphore_signal(barrier, inc=1, device_id=mate(o), device_id_type=MESH)
    count = n_pole - 1
    for d in distances:
        has_right = place + d < places
        has_left = place >= d

        @pl.when(has_right)
        def _():
            pl.semaphore_signal(barrier, inc=1, device_id=at(place + d), device_id_type=MESH)

        @pl.when(has_left)
        def _():
            pl.semaphore_signal(barrier, inc=1, device_id=at(place - d), device_id_type=MESH)

        count = count + has_right.astype(jnp.int32) + has_left.astype(jnp.int32)

    mine = pl.ds(pl.multiple_of(q * share, share), share)
    for i, block in enumerate((h_ref, o_ref, s_ref)):
        gathered[mine, i * N : (i + 1) * N] = block[0]
    pl.semaphore_wait(barrier, count)
    copies = []
    for o in range(1, n_pole):
        copy = pltpu.make_async_remote_copy(
            src_ref=gathered.at[mine], dst_ref=gathered.at[mine],
            send_sem=gs.at[o - 1], recv_sem=gr.at[o - 1],
            device_id=mate(o), device_id_type=MESH,
        )
        copy.start()
        copies.append(copy)

    iota0 = lax.broadcasted_iota(jnp.int32, (N, N), 0)
    iota1 = lax.broadcasted_iota(jnp.int32, (N, N), 1)
    one_hot = jnp.where(iota0 == order_ref[...], 1.0, 0.0)
    size = size_ref[place]
    after = size_ref[jnp.minimum(place + 1, places - 1)]
    after = jnp.where(place + 1 < places, after, 0)
    diag_mask = (iota0 < size) & (iota1 < size)
    link_mask_t = (iota0 < after) & (iota1 < size)
    padding = jnp.where((iota0 == iota1) & (iota1 >= size), 1.0, 0.0)

    for copy in copies:
        copy.wait()
    restored = dot(one_hot, gathered[...])
    coupling_t[...] = jnp.where(link_mask_t, restored[:, N : 2 * N], 0.0)

    has_right = place + 1 < places
    has_left = place >= 1
    to_right = pltpu.make_async_remote_copy(
        src_ref=coupling_t, dst_ref=link_t, send_sem=cs, recv_sem=cr,
        device_id=at(jnp.minimum(place + 1, places - 1)), device_id_type=MESH,
    )

    @pl.when(has_right)
    def _():
        to_right.start()

    for p in range(poles):
        a = restored[:, :N] + shift_ref[p] * restored[:, 2 * N :]
        a = jnp.where(diag_mask, a, 0.0) + padding
        a_all[p] = a
        work[p] = a
        d_all[p] = a
        f_all[p] = jnp.zeros((N, N), jnp.float32)

    def exists(d):
        return place + d < places, place >= d

    def neighbour(d):
        return at(jnp.minimum(place + d, places - 1)), at(jnp.maximum(place - d, 0))

    def transfer(source, target, send, recv, d, side, slot):
        return pltpu.make_async_remote_copy(
            src_ref=source.at[(side, *slot)], dst_ref=target.at[(1 - side, *slot)],
            send_sem=send.at[(side, *slot)], recv_sem=recv.at[(1 - side, *slot)],
            device_id=neighbour(d)[side], device_id_type=MESH,
        )

    def start(copies, d):
        for side, copy in copies:
            pl.when(exists(d)[side])(copy.start)

    def finish(copies, d, target, level):
        for side in (0, 1):
            @pl.when(jnp.logical_not(exists(d)[side]))
            def _():
                target[side, level] = jnp.zeros(target.shape[2:], jnp.float32)

        for side, copy in copies:
            pl.when(exists(d)[1 - side])(copy.wait_recv)
            pl.when(exists(d)[side])(copy.wait_send)

    crossing = None
    for level, d in enumerate(distances):
        invert(work, range(poles))
        if level == 0:
            @pl.when(has_left)
            def _():
                to_right.wait_recv()

            @pl.when(jnp.logical_not(has_left))
            def _():
                link_t[...] = jnp.zeros_like(link_t)

            link = link_t[...].T
            for p in range(poles):
                ul[p, :N] = coupling_t[...]
                ul[p, N:] = link
        else:
            finish(crossing, distances[level - 1], n_recv, level - 1)
            for p in range(poles):
                ul[p, :N] = n_recv[0, level - 1, p]
                ul[p, N:] = n_recv[1, level - 1, p]
        products, terms = [], []
        for p in range(poles):
            both = ul[p]
            product = dot(both, work[p])
            products.append(product)
            for side in (0, 1):
                half = slice(side * N, (side + 1) * N)
                body, diagonal = pack(dot_t(product[half], both[half]))
                t_send[side, level, p, : N // 2] = body
                t_send[side, level, p, N // 2 :] = diagonal
                copy = transfer(t_send, t_recv, ts, tr, d, side, (level, p))
                terms.append((side, copy))
                start([(side, copy)], d)
        crossing = []
        if level < levels - 1:
            for p in range(poles):
                both = ul[p]
                n_send[0, level, p] = dot_t(products[p][N:], both[:N])
                n_send[1, level, p] = dot_t(products[p][:N], both[N:])
                for side in (0, 1):
                    copy = transfer(n_send, n_recv, xs, xr, d, side, (level, p))
                    crossing.append((side, copy))
                    start([(side, copy)], d)
        finish(terms, d, t_recv, level)
        for p in range(poles):
            before = unpack(t_recv[1, level, p])
            f_all[p] += before
            left = d_all[p] - (unpack(t_recv[0, level, p]) + before)
            d_all[p] = left
            work[p] = left

    @pl.when(has_right)
    def _():
        to_right.wait_send()

    for p in range(poles):
        work[poles + p] = a_all[p] - f_all[p]
    invert(work, range(2 * poles))

    total = jnp.zeros((N, N), jnp.float32)
    for p in range(poles):
        scaled = weight_ref[p] * work[p]
        body, diagonal = pack(scaled)
        g_send[p, : N // 2] = body
        g_send[p, N // 2 :] = diagonal
        total += scaled
    to_left = pltpu.make_async_remote_copy(
        src_ref=g_send, dst_ref=g_recv, send_sem=ns, recv_sem=nr,
        device_id=at(jnp.maximum(place - 1, 0)), device_id_type=MESH,
    )

    @pl.when(has_left)
    def _():
        to_left.start()

    halves = [dot(coupling_t[...], work[poles + p]) for p in range(poles)]
    order = one_hot.T
    z_send[:, :N] = dot(order, jnp.where(diag_mask, total, 0.0))

    @pl.when(has_right)
    def _():
        to_left.wait_recv()

    @pl.when(jnp.logical_not(has_right))
    def _():
        g_recv[...] = jnp.zeros_like(g_recv)

    off_t = jnp.zeros((N, N), jnp.float32)
    for p in range(poles):
        off_t -= dot(unpack(g_recv[p]), halves[p])
    z_send[:, N:] = dot(order, jnp.where(link_mask_t, off_t, 0.0))

    copies = []
    for o in range(1, n_pole):
        theirs = pl.ds(pl.multiple_of(lax.rem(q + o, n_pole) * share, share), share)
        copy = pltpu.make_async_remote_copy(
            src_ref=z_send.at[theirs], dst_ref=z_recv.at[o - 1],
            send_sem=zs.at[o - 1], recv_sem=zr.at[o - 1],
            device_id=mate(o), device_id_type=MESH,
        )
        copy.start()
        copies.append(copy)

    @pl.when(has_left)
    def _():
        to_left.wait_send()

    result = z_send[mine]
    for o in range(1, n_pole):
        copies[o - 1].wait()
        result += z_recv[o - 1]
    diag_ref[0] = result[:, :N]
    off_ref[0] = result[:, N:]


def solution(mesh):
    n_pole, n_row, n_col = (mesh.shape[a] for a in ("pole", "row", "col"))
    places = n_row * n_col
    levels = (places - 1).bit_length()

    def per_device(h_diag, h_off, s_diag, snode_size, col_order, shifts, weights):
        poles = shifts.shape[0]
        share = h_diag.shape[2]
        h_diag, h_off, s_diag = (jnp.swapaxes(x, 1, 2) for x in (h_diag, h_off, s_diag))
        vmem = pl.BlockSpec(memory_space=pltpu.VMEM)
        smem = pl.BlockSpec(memory_space=pltpu.SMEM)
        f32 = functools.partial(lambda *shape: pltpu.VMEM(shape, jnp.float32))
        dma = pltpu.SemaphoreType.DMA
        crossings = max(levels - 1, 1)
        results = pl.pallas_call(
            functools.partial(kernel, n_pole, n_col, places, poles, levels),
            out_shape=[jax.ShapeDtypeStruct((1, share, N), jnp.float32)] * 2,
            in_specs=[vmem, vmem, vmem, smem, vmem, smem, smem],
            out_specs=[vmem, vmem],
            scratch_shapes=[
                f32(N, 3 * N), f32(N, N), f32(N, N), f32(poles, N, N),
                f32(2 * poles, N, N), f32(poles, N, N), f32(poles, N, N),
                f32(poles, 2 * N, N),
                f32(2, levels, poles, 72, N), f32(2, levels, poles, 72, N),
                f32(2, crossings, poles, N, N), f32(2, crossings, poles, N, N),
                f32(poles, 72, N), f32(poles, 72, N), f32(N, 2 * N),
                f32(n_pole - 1, share, 2 * N),
                dma((n_pole - 1,)), dma((n_pole - 1,)), dma, dma,
                dma((2, levels, poles)), dma((2, levels, poles)),
                dma((2, crossings, poles)), dma((2, crossings, poles)),
                dma, dma, dma((n_pole - 1,)), dma((n_pole - 1,)),
            ],
            compiler_params=pltpu.CompilerParams(
                collective_id=0, has_side_effects=True,
                vmem_limit_bytes=32 * 1024 * 1024,
            ),
        )(h_diag, h_off, s_diag, snode_size, col_order.reshape(1, N), shifts, weights)
        return tuple(jnp.swapaxes(x, 1, 2) for x in results)

    spread = P(("row", "col"), None, "pole")
    return jax.shard_map(
        per_device,
        mesh=mesh,
        in_specs=(spread, spread, spread, P(), P(), P("pole"), P("pole")),
        out_specs=(spread, spread),
        check_vma=False,
    )
```
